512 devices in a mesh: gx: 8 (over y_lo, core), gy: 8 (over x, y_hi), gz: 8 (over z).
Axes of the slice: x: 4, y: 8 (y_hi: 2, y_lo: 4; y = y_hi * 4 + y_lo), z: 8, core: 2. Of those that a mesh axis runs over, the one named last changes fastest.
Arguments:
- inputs: bfloat16 [448, 12288], P(('gx', 'gz'), 'gy'), may hold values from -6 to 6
- weight_in: bfloat16 [12288, 24576], P('gy', ('gx', 'gz')), may hold values from -0.0546875 to 0.0546875
- weight_out: bfloat16 [24576, 12288], P(('gx', 'gz'), 'gy'), may hold values from -0.0390625 to 0.0390625
- grad_output: bfloat16 [448, 12288], P(('gx', 'gz'), 'gy'), may hold values from -6 to 6
Outputs:
- grad_inputs: bfloat16 [448, 12288], P(('gx', 'gz'), 'gy')
- grad_weight_in: bfloat16 [12288, 24576], P('gy', ('gx', 'gz'))
- grad_weight_out: bfloat16 [24576, 12288], P(('gx', 'gz'), 'gy')
The draws below stay inside these ranges and needn't reach their ends.
All inputs are finite; a program needn't handle non-finite values.
Results may differ from the reference program's by a relative error of at most 0.0049.
Values may be sent and summed in bfloat16 or wider, within the bound.
No kernel may reach another device: no remote copies, remote signals or barrier semaphores. Data moves between devices by JAX's collectives and lax.ppermute only.
A program may use at most 64 MiB of HBM per device.

```python
import jax
import jax.numpy as jnp

D = 12288
FF = 24576
TOKENS = 448


def shard_levels(rng, dims, cuts, least, high):
    factor_of, own = 1.0, jax.random.fold_in(rng, 6)
    for axis_at, shards_of in cuts:
        heights = jnp.exp(jax.random.uniform(jax.random.fold_in(own, axis_at), (shards_of,), jnp.float32, least / len(cuts), high / len(cuts)))
        factor_of = factor_of * jnp.repeat(heights, dims[axis_at] // shards_of).reshape([-1 if axis == axis_at else 1 for axis in range(len(dims))])
    return factor_of


def normal_values(stream_key, shape, deviation, most, cuts=(), held_as=jnp.bfloat16):
    values = deviation * jax.random.normal(stream_key, shape, jnp.float32)
    if cuts:
        values = values * shard_levels(stream_key, shape, cuts, -0.22, 0.18)
    return jnp.clip(values, -most, most).astype(held_as)


def setup_inputs(seed: int = 0) -> dict:
    arg_keys = jax.random.split(jax.random.key(seed), 5)
    return {
        "inputs": normal_values(arg_keys[0], (TOKENS, D), 1.0, 6.0, ((0, 64), (1, 8))),
        "weight_in": normal_values(arg_keys[1], (D, FF), D ** -0.5, 0.0546875, ((0, 8), (1, 64))),
        "weight_out": normal_values(arg_keys[2], (FF, D), FF ** -0.5, 0.0390625, ((0, 64), (1, 8))),
        "grad_output": normal_values(arg_keys[3], (TOKENS, D), 1.0, 6.0, ((0, 64), (1, 8))),
    }


coeff = 0.7978845608


def gelu_value(v):
    inner = jnp.tanh(coeff * (v + 0.044715 * v * v * v))
    return 0.5 * v * (1.0 + inner)


def gelu_slope(v):
    inner = jnp.tanh(coeff * (v + 0.044715 * v * v * v))
    return 0.5 * (1.0 + inner) + 0.5 * v * (1.0 - inner * inner) * coeff * (1.0 + 0.134145 * v * v)


def reference(inputs, weight_in, weight_out, grad_output):
    pre = jnp.dot(inputs, weight_in, preferred_element_type=jnp.float32)
    act = gelu_value(pre).astype(jnp.bfloat16)
    dact = jnp.dot(grad_output, weight_out.T, preferred_element_type=jnp.float32)
    dpre = (dact * gelu_slope(pre)).astype(jnp.bfloat16)
    grad_weight_out = jnp.dot(act.T, grad_output, preferred_element_type=jnp.float32).astype(jnp.bfloat16)
    grad_weight_in = jnp.dot(inputs.T, dpre, preferred_element_type=jnp.float32).astype(jnp.bfloat16)
    grad_inputs = jnp.dot(dpre, weight_in.T, preferred_element_type=jnp.float32).astype(jnp.bfloat16)
    return grad_inputs, grad_weight_in, grad_weight_out
```

```python
import jax
import jax.numpy as jnp
from jax import lax
from jax.sharding import PartitionSpec as P

coeff = 0.7978845608
bf16 = jnp.bfloat16
f32 = jnp.float32


def gelu_value(v):
    inner = jnp.tanh(coeff * (v + 0.044715 * v * v * v))
    return 0.5 * v * (1.0 + inner)


def gelu_slope(v):
    inner = jnp.tanh(coeff * (v + 0.044715 * v * v * v))
    return 0.5 * (1.0 + inner) + 0.5 * v * (1.0 - inner * inner) * coeff * (1.0 + 0.134145 * v * v)


def contract_last(left, right):
    return lax.dot_general(left, right, (((1,), (1,)), ((), ())), preferred_element_type=f32)


def contract_first(left, right):
    return lax.dot_general(left, right, (((0,), (0,)), ((), ())), preferred_element_type=f32)


def per_device(inputs, weight_in, weight_out, grad_output):
    nx, ny, nz = lax.axis_size("gx"), lax.axis_size("gy"), lax.axis_size("gz")
    rows, width = inputs.shape
    hidden = weight_in.shape[1]
    chips = nx // 2 * nz
    same_core = [[x * nz + z for x in range(core, nx, 2) for z in range(nz)] for core in range(2)]
    swap_cores = [(x, x ^ 1) for x in range(nx)]

    both = jnp.concatenate([inputs, grad_output], axis=0)
    spread = jnp.broadcast_to(both[None], (chips, 2 * rows, width))
    got = lax.all_to_all(spread, ("gx", "gz"), 0, 0, axis_index_groups=same_core)
    own_in = got[:, :rows].reshape(chips * rows, width)
    own_grad = got[:, rows:].reshape(chips * rows, width)
    own = jnp.concatenate([own_in, own_grad], axis=0)
    other = lax.ppermute(own, "gx", swap_cores)
    all_in = jnp.concatenate([own_in, other[: chips * rows]], axis=0)
    all_grad = jnp.concatenate([own_grad, other[chips * rows :]], axis=0)
    tokens = 2 * chips * rows
    share = tokens // ny

    pre_part = jnp.dot(all_in, weight_in, preferred_element_type=f32).astype(bf16)
    dact_part = contract_last(all_grad, weight_out).astype(bf16)
    parts = jnp.concatenate([pre_part, dact_part], axis=1).reshape(ny, share, 2 * hidden)
    parts = lax.all_to_all(parts, "gy", 0, 0)
    sums = jnp.sum(parts.astype(f32), axis=0)
    pre, dact = sums[:, :hidden], sums[:, hidden:]
    act = gelu_value(pre).astype(bf16)
    dpre = (dact * gelu_slope(pre)).astype(bf16)
    mine = jnp.concatenate([act, dpre], axis=1)
    spread = jnp.broadcast_to(mine[None], (ny, share, 2 * hidden))
    whole = lax.all_to_all(spread, "gy", 0, 0).reshape(tokens, 2 * hidden)
    act_all, dpre_all = whole[:, :hidden], whole[:, hidden:]

    half = chips * rows
    to_other = contract_last(dpre_all[half:], weight_in)
    from_other = lax.ppermute(to_other, "gx", swap_cores)
    chip_sum = (contract_last(dpre_all[:half], weight_in) + from_other).astype(bf16)
    pieces = lax.all_to_all(
        chip_sum.reshape(chips, rows, width), ("gx", "gz"), 0, 0, axis_index_groups=same_core
    )
    grad_inputs = jnp.sum(pieces.astype(f32), axis=0).astype(bf16)
    grad_weight_out = contract_first(act_all, all_grad).astype(bf16)
    grad_weight_in = contract_first(all_in, dpre_all).astype(bf16)
    return (grad_inputs, grad_weight_in, grad_weight_out)


def solution(mesh):
    in_specs = (
        P(("gx", "gz"), "gy"),
        P("gy", ("gx", "gz")),
        P(("gx", "gz"), "gy"),
        P(("gx", "gz"), "gy"),
    )
    out_specs = (P(("gx", "gz"), "gy"), P("gy", ("gx", "gz")), P(("gx", "gz"), "gy"))
    return jax.shard_map(
        per_device, mesh=mesh, in_specs=in_specs, out_specs=out_specs, check_vma=False
    )
```

```python
import jax
import jax.numpy as jnp
from jax import lax
from jax.sharding import PartitionSpec as P

coeff = 0.7978845608
bf16 = jnp.bfloat16
f32 = jnp.float32


def gelu_value(v):
    inner = jnp.tanh(coeff * (v + 0.044715 * v * v * v))
    return 0.5 * v * (1.0 + inner)


def gelu_slope(v):
    inner = jnp.tanh(coeff * (v + 0.044715 * v * v * v))
    return 0.5 * (1.0 + inner) + 0.5 * v * (1.0 - inner * inner) * coeff * (1.0 + 0.134145 * v * v)


def contract_last(left, right):
    return lax.dot_general(left, right, (((1,), (1,)), ((), ())), preferred_element_type=f32)


def contract_first(left, right):
    return lax.dot_general(left, right, (((0,), (0,)), ((), ())), preferred_element_type=f32)


def spread_groups(ny, nz):
    def at(y, core, z):
        return (2 * y + core) * nz + z

    first = [[at(y, 0, z) for z in range(nz)] for y in range(ny)]
    second = [[at(y, 0, z) for y in range(ny)] for z in range(nz)]
    pairs = nz // ny
    first += [
        [at(y, 1, lead + dz) for y in range(ny) for dz in range(pairs)] for lead in range(0, nz, pairs)
    ]
    second += [
        [at(y, 1, pairs * k + dz) for k in range(ny)] for y in range(ny) for dz in range(pairs)
    ]
    last = [
        [at(y, 0, z) for y in range(ny) for z in range(nz)],
        [at(y, 1, pairs * k + dz) for k in range(ny) for y in range(ny) for dz in range(pairs)],
    ]
    return first, second, last


def per_device(inputs, weight_in, weight_out, grad_output):
    nx, ny, nz = lax.axis_size("gx"), lax.axis_size("gy"), lax.axis_size("gz")
    rows, width = inputs.shape
    hidden = weight_in.shape[1]
    along = nx // 2
    chips = along * nz
    first, second, last = spread_groups(along, nz)
    swap_cores = [(x, x ^ 1) for x in range(nx)]

    def swap(v):
        return lax.ppermute(v, "gx", swap_cores)

    other_in, other_out = swap(weight_in), swap(weight_out)

    both = jnp.concatenate([inputs, grad_output], axis=0)
    got = lax.all_to_all(
        jnp.broadcast_to(both[None], (nz, 2 * rows, width)), ("gx", "gz"), 0, 0, axis_index_groups=first
    ).reshape(nz * 2 * rows, width)
    got = lax.all_to_all(
        jnp.broadcast_to(got[None], (along, nz * 2 * rows, width)),
        ("gx", "gz"), 0, 0, axis_index_groups=second,
    ).reshape(chips, 2 * rows, width)
    own_in = got[:, :rows].reshape(chips * rows, width)
    own_grad = got[:, rows:].reshape(chips * rows, width)
    tokens = chips * rows
    share = tokens // (ny // 2)

    swapped_in, swapped_grad = swap(own_in), swap(own_grad)

    def shares(v):
        return v.reshape(ny // 2, 1, share, hidden)

    pre_part = jnp.concatenate(
        [
            shares(jnp.dot(own_in, weight_in, preferred_element_type=f32).astype(bf16)),
            shares(jnp.dot(own_in, other_in, preferred_element_type=f32).astype(bf16)),
        ],
        axis=1,
    )
    dact_part = jnp.concatenate(
        [
            shares(contract_last(own_grad, weight_out).astype(bf16)),
            shares(contract_last(own_grad, other_out).astype(bf16)),
        ],
        axis=1,
    )
    parts = jnp.concatenate([pre_part, dact_part], axis=3).reshape(ny, share, 2 * hidden)
    parts = lax.all_to_all(parts, "gy", 0, 0)
    sums = jnp.sum(parts.astype(f32), axis=0)
    pre, dact = sums[:, :hidden], sums[:, hidden:]
    act = gelu_value(pre).astype(bf16)
    dpre = (dact * gelu_slope(pre)).astype(bf16)
    mine = jnp.concatenate([act, dpre], axis=1)
    whole = lax.all_to_all(jnp.broadcast_to(mine[None], (ny, share, 2 * hidden)), "gy", 0, 0)
    whole = whole.reshape(ny // 2, 2, share, 2 * hidden)
    own_whole = whole[:, 0].reshape(tokens, 2 * hidden)
    for_other = whole[:, 1].reshape(tokens, 2 * hidden)
    swapped_whole = swap(for_other)

    chip_sum = contract_last(own_whole[:, hidden:], weight_in) + contract_last(for_other[:, hidden:], other_in)
    pieces = lax.all_to_all(
        chip_sum.astype(bf16).reshape(chips, rows, width), ("gx", "gz"), 0, 0, axis_index_groups=last
    )
    grad_inputs = jnp.sum(pieces.astype(f32), axis=0).astype(bf16)
    grad_weight_out = (
        contract_first(own_whole[:, :hidden], own_grad)
        + contract_first(swapped_whole[:, :hidden], swapped_grad)
    ).astype(bf16)
    grad_weight_in = (
        contract_first(own_in, own_whole[:, hidden:])
        + contract_first(swapped_in, swapped_whole[:, hidden:])
    ).astype(bf16)
    return (grad_inputs, grad_weight_in, grad_weight_out)


def solution(mesh):
    in_specs = (
        P(("gx", "gz"), "gy"),
        P("gy", ("gx", "gz")),
        P(("gx", "gz"), "gy"),
        P(("gx", "gz"), "gy"),
    )
    out_specs = (P(("gx", "gz"), "gy"), P("gy", ("gx", "gz")), P(("gx", "gz"), "gy"))
    return jax.shard_map(
        per_device, mesh=mesh, in_specs=in_specs, out_specs=out_specs, check_vma=False
    )
```

```python
import jax
import jax.numpy as jnp
from jax import lax
from jax.sharding import PartitionSpec as P

coeff = 0.7978845608
bf16 = jnp.bfloat16
f16 = jnp.float16
f32 = jnp.float32


def gelu_value(v):
    inner = jnp.tanh(coeff * (v + 0.044715 * v * v * v))
    return 0.5 * v * (1.0 + inner)


def gelu_slope(v):
    inner = jnp.tanh(coeff * (v + 0.044715 * v * v * v))
    return 0.5 * (1.0 + inner) + 0.5 * v * (1.0 - inner * inner) * coeff * (1.0 + 0.134145 * v * v)


def contract_last(left, right):
    return lax.dot_general(left, right, (((1,), (1,)), ((), ())), preferred_element_type=f32)


def contract_first(left, right):
    return lax.dot_general(left, right, (((0,), (0,)), ((), ())), preferred_element_type=f32)


def pack(sums):
    columns = sums.shape[-1]
    kinds = sums.reshape(-1, 2, columns // 2)
    most = jnp.maximum(jnp.max(jnp.abs(kinds), axis=(0, 2)), 1e-30)
    power = jnp.repeat(jnp.round(jnp.log2(most)), columns // 2)
    tail = jnp.broadcast_to(power, (*sums.shape[:-2], 8, columns))
    return jnp.concatenate([(sums * jnp.exp2(13.0 - power)).astype(f16), tail.astype(f16)], axis=-2)


def unpack(packed):
    power = packed[..., -8:-7, :].astype(f32)
    return packed[..., :-8, :].astype(f32) * jnp.exp2(power - 13.0)


class Routes:
    def __init__(self, ny, nz):
        def at(y, core, z):
            return (2 * (y % ny) + core) * nz + z % nz

        self.blocks = ny
        self.first = [[at(y, 0, z) for z in range(nz)] for y in range(ny)] + [
            [at(y, 1, z + d * ny) for y in range(ny) for d in range(nz // ny)] for z in range(ny)
        ]

        def shift(dy, dz):
            return [(at(y + dy, 0, z), at(y, 0, z)) for y in range(ny) for z in range(nz)] + [
                (at(y, 1, z + dz), at(y, 1, z)) for y in range(ny) for z in range(nz)
            ]

        far = ny // 2
        self.moves = [(b, shift(b, b if b <= far else b - ny)) for b in [far, *range(1, far), *range(far + 1, ny)]]

    def send(self, source, axes):
        return {b: lax.ppermute(source, axes, pairs) for b, pairs in self.moves}

    def send_back(self, sources, axes):
        return [lax.ppermute(sources[b], axes, [(d, s) for s, d in pairs]) for b, pairs in self.moves]


def per_device(inputs, weight_in, weight_out, grad_output):
    nx, ny, nz = lax.axis_size("gx"), lax.axis_size("gy"), lax.axis_size("gz")
    rows, width = inputs.shape
    hidden = weight_in.shape[1]
    routes = Routes(nx // 2, nz)
    blocks = routes.blocks
    swap_cores = [(x, x ^ 1) for x in range(nx)]

    def swap(v):
        return lax.ppermute(v, "gx", swap_cores)

    halves = 2
    same_half = [[x * halves + h for x in range(ny // halves)] for h in range(halves)]
    other_half = [(g, g ^ 1) for g in range(ny)]

    both = jnp.concatenate([inputs, grad_output], axis=0)
    near = lax.all_to_all(
        jnp.broadcast_to(both[None], (nz, 2 * rows, width)), ("gx", "gz"), 0, 0, axis_index_groups=routes.first
    )
    share = nz * rows
    near = jnp.concatenate(
        [near[:, :rows].reshape(share, width), near[:, rows:].reshape(share, width)], axis=1
    )
    chip_in = jnp.concatenate([weight_in, swap(weight_in)], axis=1)
    chip_out = jnp.concatenate([weight_out, swap(weight_out)], axis=0)
    chip_in, chip_out = lax.optimization_barrier((chip_in, chip_out))
    found = routes.send(near, ("gx", "gz"))
    own = jnp.concatenate([near] + [found[b] for b in range(1, blocks)], axis=0)
    own_in, own_grad = own[:, :width], own[:, width:]
    swapped = swap(own)
    tokens = blocks * share

    pre_part = jnp.dot(own_in, chip_in, preferred_element_type=f32)
    dact_part = contract_last(own_grad, chip_out)
    parts = pack(jnp.concatenate([pre_part, dact_part], axis=1).reshape(blocks, share, 4 * hidden))
    parts = lax.all_to_all(parts, "gy", 0, 0, axis_index_groups=same_half)
    sums = jnp.sum(unpack(parts), axis=0)
    sums = sums + unpack(lax.ppermute(pack(sums), "gy", other_half))
    pre, dact = sums[:, : 2 * hidden], sums[:, 2 * hidden :]
    act = gelu_value(pre).astype(bf16)
    dpre = (dact * gelu_slope(pre)).astype(bf16)
    mine = jnp.concatenate([act, dpre], axis=1)
    whole = lax.all_to_all(
        jnp.broadcast_to(mine[None], (blocks, share, 4 * hidden)), "gy", 0, 0, axis_index_groups=same_half
    ).reshape(tokens, 4 * hidden)
    act_own, act_other = whole[:, :hidden], whole[:, hidden : 2 * hidden]
    dpre_own, dpre_other = whole[:, 2 * hidden : 3 * hidden], whole[:, 3 * hidden :]

    chip_sum = contract_last(whole[:, 2 * hidden :], chip_in).astype(bf16)
    for_other, chip_sum = lax.optimization_barrier(
        (jnp.concatenate([act_other, dpre_other], axis=1), chip_sum)
    )
    chip_sum = chip_sum.reshape(blocks, share, width)
    total = chip_sum[0].astype(f32)
    for v in routes.send_back(chip_sum, ("gx", "gz")):
        total = total + v.astype(f32)
    swapped_whole = swap(for_other)
    pieces = lax.all_to_all(
        total.astype(bf16).reshape(nz, rows, width), ("gx", "gz"), 0, 0, axis_index_groups=routes.first
    )
    grad_inputs = jnp.sum(pieces.astype(f32), axis=0).astype(bf16)
    grad_weight_out = (
        contract_first(act_own, own_grad) + contract_first(swapped_whole[:, :hidden], swapped[:, width:])
    ).astype(bf16)
    grad_weight_in = (
        contract_first(own_in, dpre_own) + contract_first(swapped[:, :width], swapped_whole[:, hidden:])
    ).astype(bf16)
    return (grad_inputs, grad_weight_in, grad_weight_out)


def solution(mesh):
    in_specs = (
        P(("gx", "gz"), "gy"),
        P("gy", ("gx", "gz")),
        P(("gx", "gz"), "gy"),
        P(("gx", "gz"), "gy"),
    )
    out_specs = (P(("gx", "gz"), "gy"), P("gy", ("gx", "gz")), P(("gx", "gz"), "gy"))
    return jax.shard_map(
        per_device, mesh=mesh, in_specs=in_specs, out_specs=out_specs, check_vma=False
    )
```

```python
import jax
import jax.numpy as jnp
from jax import lax
from jax.experimental import pallas as pl
from jax.experimental.pallas import tpu as pltpu
from jax.sharding import PartitionSpec as P

coeff = 0.7978845608
bf16 = jnp.bfloat16
f32 = jnp.float32


def gelu_value(v):
    inner = jnp.tanh(coeff * (v + 0.044715 * v * v * v))
    return 0.5 * v * (1.0 + inner)


def gelu_slope(v):
    inner = jnp.tanh(coeff * (v + 0.044715 * v * v * v))
    return 0.5 * (1.0 + inner) + 0.5 * v * (1.0 - inner * inner) * coeff * (1.0 + 0.134145 * v * v)


def contract_last(left, right):
    return lax.dot_general(left, right, (((1,), (1,)), ((), ())), preferred_element_type=f32)


def contract_first(left, right):
    return lax.dot_general(left, right, (((0,), (0,)), ((), ())), preferred_element_type=f32)


def first_products(
    own_ref, in0, in1, out0, out1, parts_ref, mine_ref, kept_in, kept_grad, held_in, held_out, total, sems
):
    width, hidden = in0.shape
    blocks, share, _ = parts_ref.shape
    copies = [
        pltpu.make_async_copy(in0, held_in.at[:, :hidden], sems.at[0]),
        pltpu.make_async_copy(in1, held_in.at[:, hidden:], sems.at[1]),
        pltpu.make_async_copy(out0, held_out.at[:hidden], sems.at[2]),
        pltpu.make_async_copy(out1, held_out.at[hidden:], sems.at[3]),
        pltpu.make_async_copy(own_ref.at[:, :width], kept_in, sems.at[4]),
        pltpu.make_async_copy(own_ref.at[:, width:], kept_grad, sems.at[5]),
    ]
    for copy in copies:
        copy.start()

    def put(product, columns):
        total[:, columns] = product
        for b in range(blocks):
            parts_ref[b, :, columns] = product[b * share : (b + 1) * share].astype(bf16)

    copies[0].wait()
    copies[1].wait()
    put(jnp.dot(own_ref[:, :width], held_in[...], preferred_element_type=f32), slice(0, 2 * hidden))
    copies[2].wait()
    copies[3].wait()
    put(contract_last(own_ref[:, width:], held_out[...]), slice(2 * hidden, 4 * hidden))
    block = lax.div(lax.axis_index("gy"), lax.div(lax.axis_size("gy"), blocks))
    mine_ref[...] = total[pl.ds(pl.multiple_of(block * share, share), share), :]
    parts_ref[block] = jnp.zeros((share, 4 * hidden), bf16)
    copies[4].wait()
    copies[5].wait()


def last_product(whole_ref, in0, in1, rounded_ref, mine_ref, other_ref, held, sems):
    width, hidden = in0.shape
    blocks, share, _ = rounded_ref.shape
    copies = [
        pltpu.make_async_copy(in0, held.at[:, :hidden], sems.at[0]),
        pltpu.make_async_copy(in1, held.at[:, hidden:], sems.at[1]),
    ]
    for copy in copies:
        copy.start()
    other_ref[:, :hidden] = whole_ref[:, hidden : 2 * hidden]
    other_ref[:, hidden:] = whole_ref[:, 3 * hidden :]
    for copy in copies:
        copy.wait()
    product = contract_last(whole_ref[:, 2 * hidden :], held[...])
    for b in range(blocks):
        rounded_ref[b] = product[b * share : (b + 1) * share].astype(bf16)
    mine_ref[...] = product[:share]


class Routes:
    def __init__(self, ny, nz):
        def at(y, core, z):
            return (2 * (y % ny) + core) * nz + z % nz

        self.blocks = ny
        self.first = [[at(y, 0, z) for z in range(nz)] for y in range(ny)] + [
            [at(y, 1, z + d * ny) for y in range(ny) for d in range(nz // ny)] for z in range(ny)
        ]

        def shift(dy, dz):
            return [(at(y + dy, 0, z), at(y, 0, z)) for y in range(ny) for z in range(nz)] + [
                (at(y, 1, z + dz), at(y, 1, z)) for y in range(ny) for z in range(nz)
            ]

        far = ny // 2
        self.moves = [(b, shift(b, b if b <= far else b - ny)) for b in [far, *range(1, far), *range(far + 1, ny)]]

    def send(self, source, axes):
        return {b: lax.ppermute(source, axes, pairs) for b, pairs in self.moves}

    def send_back(self, sources, axes):
        return [lax.ppermute(sources[b], axes, [(d, s) for s, d in pairs]) for b, pairs in self.moves]


def per_device(inputs, weight_in, weight_out, grad_output):
    nx, ny, nz = lax.axis_size("gx"), lax.axis_size("gy"), lax.axis_size("gz")
    rows, width = inputs.shape
    hidden = weight_in.shape[1]
    routes = Routes(nx // 2, nz)
    blocks = routes.blocks
    swap_cores = [(x, x ^ 1) for x in range(nx)]

    def swap(v):
        return lax.ppermute(v, "gx", swap_cores)

    halves = 2
    same_half = [[x * halves + h for x in range(ny // halves)] for h in range(halves)]
    other_half = [(g, g ^ 1) for g in range(ny)]

    both = jnp.concatenate([inputs, grad_output], axis=0)
    near = lax.all_to_all(
        jnp.broadcast_to(both[None], (nz, 2 * rows, width)), ("gx", "gz"), 0, 0, axis_index_groups=routes.first
    )
    share = nz * rows
    near = jnp.concatenate(
        [near[:, :rows].reshape(share, width), near[:, rows:].reshape(share, width)], axis=1
    )
    other_in, other_out = swap(weight_in), swap(weight_out)
    found = routes.send(near, ("gx", "gz"))
    found = [near] + [found[b] for b in range(1, blocks)]
    own = jnp.concatenate(found, axis=0)
    tokens = blocks * share

    vmem, anywhere = pl.BlockSpec(memory_space=pltpu.VMEM), pl.BlockSpec(memory_space=pl.ANY)
    mib = 1024 * 1024
    parts, mine, kept_in, kept_grad = pl.pallas_call(
        first_products,
        out_shape=(
            jax.ShapeDtypeStruct((blocks, share, 4 * hidden), bf16),
            jax.ShapeDtypeStruct((share, 4 * hidden), f32),
            jax.ShapeDtypeStruct((tokens, width), bf16),
            jax.ShapeDtypeStruct((tokens, width), bf16),
        ),
        in_specs=[vmem] + [anywhere] * 4,
        out_specs=(vmem, vmem, anywhere, anywhere),
        scratch_shapes=[
            pltpu.VMEM((width, 2 * hidden), bf16),
            pltpu.VMEM((2 * hidden, width), bf16),
            pltpu.VMEM((tokens, 4 * hidden), f32),
            pltpu.SemaphoreType.DMA((6,)),
        ],
        compiler_params=pltpu.CompilerParams(vmem_limit_bytes=14 * mib),
        cost_estimate=pl.CostEstimate(
            flops=8 * tokens * width * hidden, bytes_accessed=8 * width * hidden, transcendentals=0
        ),
    )(own, weight_in, other_in, weight_out, other_out)
    swapped_in, swapped_grad = swap(kept_in), swap(kept_grad)
    parts = lax.all_to_all(parts, "gy", 0, 0, axis_index_groups=same_half)
    sums = mine + jnp.sum(parts.astype(f32), axis=0)
    sums = sums + lax.ppermute(sums.astype(bf16), "gy", other_half).astype(f32)
    pre, dact = sums[:, : 2 * hidden], sums[:, 2 * hidden :]
    act = gelu_value(pre).astype(bf16)
    dpre = (dact * gelu_slope(pre)).astype(bf16)
    done = jnp.concatenate([act, dpre], axis=1)
    whole = lax.all_to_all(
        jnp.broadcast_to(done[None], (blocks, share, 4 * hidden)), "gy", 0, 0, axis_index_groups=same_half
    ).reshape(tokens, 4 * hidden)
    rounded, total, for_other = pl.pallas_call(
        last_product,
        out_shape=(
            jax.ShapeDtypeStruct((blocks, share, width), bf16),
            jax.ShapeDtypeStruct((share, width), f32),
            jax.ShapeDtypeStruct((tokens, 2 * hidden), bf16),
        ),
        in_specs=[vmem, anywhere, anywhere],
        out_specs=(vmem, vmem, vmem),
        scratch_shapes=[pltpu.VMEM((width, 2 * hidden), bf16), pltpu.SemaphoreType.DMA((2,))],
        compiler_params=pltpu.CompilerParams(vmem_limit_bytes=10 * mib),
        cost_estimate=pl.CostEstimate(
            flops=4 * tokens * width * hidden, bytes_accessed=4 * width * hidden, transcendentals=0
        ),
    )(whole, weight_in, other_in)
    for v in routes.send_back(rounded, ("gx", "gz")):
        total = total + v.astype(f32)
    swapped_whole = swap(for_other)
    pieces = lax.all_to_all(
        total.astype(bf16).reshape(nz, rows, width), ("gx", "gz"), 0, 0, axis_index_groups=routes.first
    )
    grad_inputs = jnp.sum(pieces.astype(f32), axis=0).astype(bf16)
    grad_weight_out = contract_first(
        jnp.concatenate([whole[:, :hidden], swapped_whole[:, :hidden]], axis=0),
        jnp.concatenate([kept_grad, swapped_grad], axis=0),
    ).astype(bf16)
    grad_weight_in = contract_first(
        jnp.concatenate([kept_in, swapped_in], axis=0),
        jnp.concatenate([whole[:, 2 * hidden : 3 * hidden], swapped_whole[:, hidden:]], axis=0),
    ).astype(bf16)
    return (grad_inputs, grad_weight_in, grad_weight_out)


def solution(mesh):
    in_specs = (
        P(("gx", "gz"), "gy"),
        P("gy", ("gx", "gz")),
        P(("gx", "gz"), "gy"),
        P(("gx", "gz"), "gy"),
    )
    out_specs = (P(("gx", "gz"), "gy"), P("gy", ("gx", "gz")), P(("gx", "gz"), "gy"))
    return jax.shard_map(
        per_device, mesh=mesh, in_specs=in_specs, out_specs=out_specs, check_vma=False
    )
```

```python
import jax
import jax.numpy as jnp
from jax import lax
from jax.experimental import pallas as pl
from jax.experimental.pallas import tpu as pltpu
from jax.sharding import PartitionSpec as P

coeff = 0.7978845608
bf16 = jnp.bfloat16
f32 = jnp.float32


def gelu_value(v):
    inner = jnp.tanh(coeff * (v + 0.044715 * v * v * v))
    return 0.5 * v * (1.0 + inner)


def gelu_slope(v):
    inner = jnp.tanh(coeff * (v + 0.044715 * v * v * v))
    return 0.5 * (1.0 + inner) + 0.5 * v * (1.0 - inner * inner) * coeff * (1.0 + 0.134145 * v * v)


def contract_last(left, right):
    return lax.dot_general(left, right, (((1,), (1,)), ((), ())), preferred_element_type=f32)


def contract_first(left, right):
    return lax.dot_general(left, right, (((0,), (0,)), ((), ())), preferred_element_type=f32)


def first_products(
    own_ref, in0, in1, out0, out1, parts_ref, mine_ref, kept_in, kept_grad, held_in, held_out, total, sems
):
    width, hidden = in0.shape
    blocks, share, _ = parts_ref.shape
    copies = [
        pltpu.make_async_copy(in0, held_in.at[:, :hidden], sems.at[0]),
        pltpu.make_async_copy(in1, held_in.at[:, hidden:], sems.at[1]),
        pltpu.make_async_copy(out0, held_out.at[:hidden], sems.at[2]),
        pltpu.make_async_copy(out1, held_out.at[hidden:], sems.at[3]),
        pltpu.make_async_copy(own_ref.at[:, :width], kept_in, sems.at[4]),
        pltpu.make_async_copy(own_ref.at[:, width:], kept_grad, sems.at[5]),
    ]
    for copy in copies:
        copy.start()

    def put(product, columns):
        total[:, columns] = product
        for b in range(blocks):
            parts_ref[b, :, columns] = product[b * share : (b + 1) * share].astype(bf16)

    copies[0].wait()
    copies[1].wait()
    put(jnp.dot(own_ref[:, :width], held_in[...], preferred_element_type=f32), slice(0, 2 * hidden))
    copies[2].wait()
    copies[3].wait()
    put(contract_last(own_ref[:, width:], held_out[...]), slice(2 * hidden, 4 * hidden))
    block = lax.div(lax.axis_index("gy"), lax.div(lax.axis_size("gy"), blocks))
    mine_ref[...] = total[pl.ds(pl.multiple_of(block * share, share), share), :]
    parts_ref[block] = jnp.zeros((share, 4 * hidden), bf16)
    copies[4].wait()
    copies[5].wait()


def last_product(whole_ref, in0, in1, rounded_ref, mine_ref, other_ref, held, sems):
    width, hidden = in0.shape
    blocks, share, _ = rounded_ref.shape
    copies = [
        pltpu.make_async_copy(in0, held.at[:, :hidden], sems.at[0]),
        pltpu.make_async_copy(in1, held.at[:, hidden:], sems.at[1]),
    ]
    for copy in copies:
        copy.start()
    other_ref[:, :hidden] = whole_ref[:, hidden : 2 * hidden]
    other_ref[:, hidden:] = whole_ref[:, 3 * hidden :]
    for copy in copies:
        copy.wait()
    product = contract_last(whole_ref[:, 2 * hidden :], held[...])
    for b in range(blocks):
        rounded_ref[b] = product[b * share : (b + 1) * share].astype(bf16)
    mine_ref[...] = product[:share]


class Routes:
    def __init__(self, ny, nz):
        def at(y, core, z):
            return (2 * (y % ny) + core) * nz + z % nz

        self.blocks = ny
        self.first = [[at(y, 0, z) for z in range(nz)] for y in range(ny)] + [
            [at(y, 1, z + d * ny) for y in range(ny) for d in range(nz // ny)] for z in range(ny)
        ]

        def move(b):
            step = b if b <= ny // 2 else b - ny
            return [(at(y ^ b, 0, z), at(y, 0, z)) for y in range(ny) for z in range(nz)] + [
                (at(y, 1, z + step), at(y, 1, z)) for y in range(ny) for z in range(nz)
            ]

        far = ny // 2
        self.moves = [(b, move(b)) for b in [far, *range(ny - 1, far, -1), *range(1, far)]]

    def send(self, source, axes):
        return {b: lax.ppermute(source, axes, pairs) for b, pairs in self.moves}

    def send_back(self, sources, axes):
        return [lax.ppermute(sources[b], axes, [(d, s) for s, d in pairs]) for b, pairs in self.moves]


def per_device(inputs, weight_in, weight_out, grad_output):
    nx, ny, nz = lax.axis_size("gx"), lax.axis_size("gy"), lax.axis_size("gz")
    rows, width = inputs.shape
    hidden = weight_in.shape[1]
    routes = Routes(nx // 2, nz)
    blocks = routes.blocks
    swap_cores = [(x, x ^ 1) for x in range(nx)]

    def swap(v):
        return lax.ppermute(v, "gx", swap_cores)

    halves = 2
    same_half = [[x * halves + h for x in range(ny // halves)] for h in range(halves)]
    other_half = [(g, g ^ 1) for g in range(ny)]

    both = jnp.concatenate([inputs, grad_output], axis=0)
    near = lax.all_to_all(
        jnp.broadcast_to(both[None], (nz, 2 * rows, width)), ("gx", "gz"), 0, 0, axis_index_groups=routes.first
    )
    share = nz * rows
    near = jnp.concatenate(
        [near[:, :rows].reshape(share, width), near[:, rows:].reshape(share, width)], axis=1
    )
    other_in, other_out = swap(weight_in), swap(weight_out)
    found = routes.send(near, ("gx", "gz"))
    found = [near] + [found[b] for b in range(1, blocks)]
    own = jnp.concatenate(found, axis=0)
    tokens = blocks * share

    vmem, anywhere = pl.BlockSpec(memory_space=pltpu.VMEM), pl.BlockSpec(memory_space=pl.ANY)
    mib = 1024 * 1024
    parts, mine, kept_in, kept_grad = pl.pallas_call(
        first_products,
        out_shape=(
            jax.ShapeDtypeStruct((blocks, share, 4 * hidden), bf16),
            jax.ShapeDtypeStruct((share, 4 * hidden), f32),
            jax.ShapeDtypeStruct((tokens, width), bf16),
            jax.ShapeDtypeStruct((tokens, width), bf16),
        ),
        in_specs=[vmem] + [anywhere] * 4,
        out_specs=(vmem, vmem, anywhere, anywhere),
        scratch_shapes=[
            pltpu.VMEM((width, 2 * hidden), bf16),
            pltpu.VMEM((2 * hidden, width), bf16),
            pltpu.VMEM((tokens, 4 * hidden), f32),
            pltpu.SemaphoreType.DMA((6,)),
        ],
        compiler_params=pltpu.CompilerParams(vmem_limit_bytes=14 * mib),
        cost_estimate=pl.CostEstimate(
            flops=8 * tokens * width * hidden, bytes_accessed=8 * width * hidden, transcendentals=0
        ),
    )(own, weight_in, other_in, weight_out, other_out)
    swapped_in, swapped_grad = swap(kept_in), swap(kept_grad)
    parts = lax.all_to_all(parts, "gy", 0, 0, axis_index_groups=same_half)
    sums = mine + jnp.sum(parts.astype(f32), axis=0)
    sums = sums + lax.ppermute(sums.astype(bf16), "gy", other_half).astype(f32)
    pre, dact = sums[:, : 2 * hidden], sums[:, 2 * hidden :]
    act = gelu_value(pre).astype(bf16)
    dpre = (dact * gelu_slope(pre)).astype(bf16)
    done = jnp.concatenate([act, dpre], axis=1)
    whole = lax.all_to_all(
        jnp.broadcast_to(done[None], (blocks, share, 4 * hidden)), "gy", 0, 0, axis_index_groups=same_half
    ).reshape(tokens, 4 * hidden)
    rounded, total, for_other = pl.pallas_call(
        last_product,
        out_shape=(
            jax.ShapeDtypeStruct((blocks, share, width), bf16),
            jax.ShapeDtypeStruct((share, width), f32),
            jax.ShapeDtypeStruct((tokens, 2 * hidden), bf16),
        ),
        in_specs=[vmem, anywhere, anywhere],
        out_specs=(vmem, vmem, vmem),
        scratch_shapes=[pltpu.VMEM((width, 2 * hidden), bf16), pltpu.SemaphoreType.DMA((2,))],
        compiler_params=pltpu.CompilerParams(vmem_limit_bytes=10 * mib),
        cost_estimate=pl.CostEstimate(
            flops=4 * tokens * width * hidden, bytes_accessed=4 * width * hidden, transcendentals=0
        ),
    )(whole, weight_in, other_in)
    for v in routes.send_back(rounded, ("gx", "gz")):
        total = total + v.astype(f32)
    swapped_whole = swap(for_other)
    pieces = lax.all_to_all(
        total.astype(bf16).reshape(nz, rows, width), ("gx", "gz"), 0, 0, axis_index_groups=routes.first
    )
    grad_inputs = jnp.sum(pieces.astype(f32), axis=0).astype(bf16)
    grad_weight_out = contract_first(
        jnp.concatenate([whole[:, :hidden], swapped_whole[:, :hidden]], axis=0),
        jnp.concatenate([kept_grad, swapped_grad], axis=0),
    ).astype(bf16)
    grad_weight_in = contract_first(
        jnp.concatenate([kept_in, swapped_in], axis=0),
        jnp.concatenate([whole[:, 2 * hidden : 3 * hidden], swapped_whole[:, hidden:]], axis=0),
    ).astype(bf16)
    return (grad_inputs, grad_weight_in, grad_weight_out)


def solution(mesh):
    in_specs = (
        P(("gx", "gz"), "gy"),
        P("gy", ("gx", "gz")),
        P(("gx", "gz"), "gy"),
        P(("gx", "gz"), "gy"),
    )
    out_specs = (P(("gx", "gz"), "gy"), P("gy", ("gx", "gz")), P(("gx", "gz"), "gy"))
    return jax.shard_map(
        per_device, mesh=mesh, in_specs=in_specs, out_specs=out_specs, check_vma=False
    )
```

```python
import jax
import jax.numpy as jnp
from jax import lax
from jax.experimental import pallas as pl
from jax.experimental.pallas import tpu as pltpu
from jax.sharding import PartitionSpec as P

coeff = 0.7978845608
bf16 = jnp.bfloat16
f32 = jnp.float32


def gelu_value(v):
    inner = jnp.tanh(coeff * (v + 0.044715 * v * v * v))
    return 0.5 * v * (1.0 + inner)


def gelu_slope(v):
    inner = jnp.tanh(coeff * (v + 0.044715 * v * v * v))
    return 0.5 * (1.0 + inner) + 0.5 * v * (1.0 - inner * inner) * coeff * (1.0 + 0.134145 * v * v)


def contract_last(left, right):
    return lax.dot_general(left, right, (((1,), (1,)), ((), ())), preferred_element_type=f32)


def contract_first(left, right):
    return lax.dot_general(left, right, (((0,), (0,)), ((), ())), preferred_element_type=f32)


def first_products(
    own_ref, in0, in1, out0, out1, parts_ref, mine_ref, kept_ref, held_in, held_out, total, sems
):
    width, hidden = in0.shape
    blocks, share, _ = parts_ref.shape
    copies = [
        pltpu.make_async_copy(in0, held_in.at[:, :hidden], sems.at[0]),
        pltpu.make_async_copy(in1, held_in.at[:, hidden:], sems.at[1]),
        pltpu.make_async_copy(out0, held_out.at[:hidden], sems.at[2]),
        pltpu.make_async_copy(out1, held_out.at[hidden:], sems.at[3]),
        pltpu.make_async_copy(own_ref.at[:, :width], kept_ref.at[0], sems.at[4]),
        pltpu.make_async_copy(own_ref.at[:, width:], kept_ref.at[1], sems.at[5]),
    ]
    for copy in copies:
        copy.start()

    def put(product, columns):
        total[:, columns] = product
        for b in range(blocks):
            parts_ref[b, :, columns] = product[b * share : (b + 1) * share].astype(bf16)

    copies[0].wait()
    copies[1].wait()
    put(jnp.dot(own_ref[:, :width], held_in[...], preferred_element_type=f32), slice(0, 2 * hidden))
    copies[2].wait()
    copies[3].wait()
    put(contract_last(own_ref[:, width:], held_out[...]), slice(2 * hidden, 4 * hidden))
    block = lax.div(lax.axis_index("gy"), lax.div(lax.axis_size("gy"), blocks))
    mine_ref[...] = total[pl.ds(pl.multiple_of(block * share, share), share), :]
    parts_ref[block] = jnp.zeros((share, 4 * hidden), bf16)
    copies[4].wait()
    copies[5].wait()


def last_product(whole_ref, in0, in1, rounded_ref, mine_ref, other_ref, held, sems):
    width, hidden = in0.shape
    blocks, share, _ = rounded_ref.shape
    copies = [
        pltpu.make_async_copy(in0, held.at[:, :hidden], sems.at[0]),
        pltpu.make_async_copy(in1, held.at[:, hidden:], sems.at[1]),
    ]
    for copy in copies:
        copy.start()
    other_ref[:, :hidden] = whole_ref[:, hidden : 2 * hidden]
    other_ref[:, hidden:] = whole_ref[:, 3 * hidden :]
    for copy in copies:
        copy.wait()
    product = contract_last(whole_ref[:, 2 * hidden :], held[...])
    for b in range(blocks):
        rounded_ref[b] = product[b * share : (b + 1) * share].astype(bf16)
    mine_ref[...] = product[:share]


class Routes:
    def __init__(self, ny, nz):
        def at(y, core, z):
            return (2 * (y % ny) + core) * nz + z % nz

        self.blocks = ny
        self.first = [[at(y, 0, z) for z in range(nz)] for y in range(ny)] + [
            [at(y, 1, z + d * ny) for y in range(ny) for d in range(nz // ny)] for z in range(ny)
        ]

        def move(b):
            step = b if b <= ny // 2 else b - ny
            return [(at(y ^ b, 0, z), at(y, 0, z)) for y in range(ny) for z in range(nz)] + [
                (at(y, 1, z + step), at(y, 1, z)) for y in range(ny) for z in range(nz)
            ]

        far = ny // 2
        self.moves = [(b, move(b)) for b in [far, *range(ny - 1, far, -1), *range(1, far)]]

    def send(self, source, axes):
        return {b: lax.ppermute(source, axes, pairs) for b, pairs in self.moves}

    def send_back(self, sources, axes):
        return [lax.ppermute(sources[b], axes, [(d, s) for s, d in pairs]) for b, pairs in self.moves]


def per_device(inputs, weight_in, weight_out, grad_output):
    nx, ny, nz = lax.axis_size("gx"), lax.axis_size("gy"), lax.axis_size("gz")
    rows, width = inputs.shape
    hidden = weight_in.shape[1]
    routes = Routes(nx // 2, nz)
    blocks = routes.blocks
    swap_cores = [(x, x ^ 1) for x in range(nx)]

    def swap(v):
        return lax.ppermute(v, "gx", swap_cores)

    halves = 2
    same_half = [[x * halves + h for x in range(ny // halves)] for h in range(halves)]
    other_half = [(g, g ^ 1) for g in range(ny)]

    both = jnp.concatenate([inputs, grad_output], axis=0)
    near = lax.all_to_all(
        jnp.broadcast_to(both[None], (nz, 2 * rows, width)), ("gx", "gz"), 0, 0, axis_index_groups=routes.first
    )
    share = nz * rows
    near = jnp.concatenate(
        [near[:, :rows].reshape(share, width), near[:, rows:].reshape(share, width)], axis=1
    )
    other_in, other_out = swap(weight_in), swap(weight_out)
    found = routes.send(near, ("gx", "gz"))
    found = [near] + [found[b] for b in range(1, blocks)]
    own = jnp.concatenate(found, axis=0)
    tokens = blocks * share

    vmem, anywhere = pl.BlockSpec(memory_space=pltpu.VMEM), pl.BlockSpec(memory_space=pl.ANY)
    mib = 1024 * 1024
    parts, mine, kept = pl.pallas_call(
        first_products,
        out_shape=(
            jax.ShapeDtypeStruct((blocks, share, 4 * hidden), bf16),
            jax.ShapeDtypeStruct((share, 4 * hidden), f32),
            jax.ShapeDtypeStruct((2, tokens, width), bf16),
        ),
        in_specs=[vmem] + [anywhere] * 4,
        out_specs=(vmem, vmem, anywhere),
        scratch_shapes=[
            pltpu.VMEM((width, 2 * hidden), bf16),
            pltpu.VMEM((2 * hidden, width), bf16),
            pltpu.VMEM((tokens, 4 * hidden), f32),
            pltpu.SemaphoreType.DMA((6,)),
        ],
        compiler_params=pltpu.CompilerParams(vmem_limit_bytes=14 * mib),
        cost_estimate=pl.CostEstimate(
            flops=8 * tokens * width * hidden, bytes_accessed=8 * width * hidden, transcendentals=0
        ),
    )(own, weight_in, other_in, weight_out, other_out)
    swapped = swap(kept)
    parts = lax.all_to_all(parts, "gy", 0, 0, axis_index_groups=same_half)
    sums = mine + jnp.sum(parts.astype(f32), axis=0)
    sums = sums + lax.ppermute(sums.astype(bf16), "gy", other_half).astype(f32)
    pre, dact = sums[:, : 2 * hidden], sums[:, 2 * hidden :]
    act = gelu_value(pre).astype(bf16)
    dpre = (dact * gelu_slope(pre)).astype(bf16)
    done = jnp.concatenate([act, dpre], axis=1)
    whole = lax.all_to_all(
        jnp.broadcast_to(done[None], (blocks, share, 4 * hidden)), "gy", 0, 0, axis_index_groups=same_half
    ).reshape(tokens, 4 * hidden)
    rounded, total, for_other = pl.pallas_call(
        last_product,
        out_shape=(
            jax.ShapeDtypeStruct((blocks, share, width), bf16),
            jax.ShapeDtypeStruct((share, width), f32),
            jax.ShapeDtypeStruct((tokens, 2 * hidden), bf16),
        ),
        in_specs=[vmem, anywhere, anywhere],
        out_specs=(vmem, vmem, vmem),
        scratch_shapes=[pltpu.VMEM((width, 2 * hidden), bf16), pltpu.SemaphoreType.DMA((2,))],
        compiler_params=pltpu.CompilerParams(vmem_limit_bytes=10 * mib),
        cost_estimate=pl.CostEstimate(
            flops=4 * tokens * width * hidden, bytes_accessed=4 * width * hidden, transcendentals=0
        ),
    )(whole, weight_in, other_in)
    for v in routes.send_back(rounded, ("gx", "gz")):
        total = total + v.astype(f32)
    swapped_whole = swap(for_other)
    pieces = lax.all_to_all(
        total.astype(bf16).reshape(nz, rows, width), ("gx", "gz"), 0, 0, axis_index_groups=routes.first
    )
    grad_inputs = jnp.sum(pieces.astype(f32), axis=0).astype(bf16)
    grad_weight_out = contract_first(
        jnp.concatenate([whole[:, :hidden], swapped_whole[:, :hidden]], axis=0),
        jnp.concatenate([kept[1], swapped[1]], axis=0),
    ).astype(bf16)
    grad_weight_in = contract_first(
        jnp.concatenate([kept[0], swapped[0]], axis=0),
        jnp.concatenate([whole[:, 2 * hidden : 3 * hidden], swapped_whole[:, hidden:]], axis=0),
    ).astype(bf16)
    return (grad_inputs, grad_weight_in, grad_weight_out)


def solution(mesh):
    in_specs = (
        P(("gx", "gz"), "gy"),
        P("gy", ("gx", "gz")),
        P(("gx", "gz"), "gy"),
        P(("gx", "gz"), "gy"),
    )
    out_specs = (P(("gx", "gz"), "gy"), P("gy", ("gx", "gz")), P(("gx", "gz"), "gy"))
    return jax.shard_map(
        per_device, mesh=mesh, in_specs=in_specs, out_specs=out_specs, check_vma=False
    )
```
